512 devices in a mesh: row: 32 (over z_hi, y, core), col: 16 (over x, z_lo).
Axes of the slice: x: 4, y: 8, z: 8 (z_hi: 2, z_lo: 4; z = z_hi * 4 + z_lo), core: 2. Of those that a mesh axis runs over, the one named last changes fastest.
Arguments:
- matrix: float32 [16384, 16384], P('row', 'col'), as said below
- lower_inverse: float32 [256, 256], replicated, as said below
- rhs: float32 [16384, 512], P('row', 'col'), may hold values from -6 to 6
- sources: int32 [512], P('col'), may hold values from 0 to 16383
Outputs:
- updated: float32 [16384, 16384], P('row', 'col')
- rhs_out: float32 [16384, 512], P('row', 'col')
The draws below stay inside these ranges and needn't reach their ends.
Inputs may be any that keep to these rules, and one draw needn't show every extreme that they name: matrix is exactly symmetric. lower_inverse is lower triangular with a positive diagonal; it is drawn independently of matrix and need not be the inverse factor of matrix's diagonal block.
All inputs are finite; a program needn't handle non-finite values.
Results may differ from the reference program's by a relative error of at most 0.00005.
Values sent between devices are 32-bit elements; how exact they have to be, the bound alone decides.
A program may use at most 64 MiB of HBM per device.

```python
import jax
import jax.numpy as jnp
from jax import lax

W = 16384
B = 256
R = 512


def draw_matrix(key, part):
    key = jax.random.fold_in(key, 11)
    noise_key, diag_key = jax.random.split(key)
    noise = 0.7 * jax.random.normal(noise_key, (W, W), jnp.float32)
    symmetric = 0.5 * (noise + noise.T)
    diag_vals = 4.0 + 4.0 * jax.random.uniform(diag_key, (W,), jnp.float32)
    row_ids = jnp.arange(W, dtype=jnp.int32)
    on_diag = row_ids[:, None] == row_ids[None, :]
    return jnp.where(on_diag, diag_vals[None, :], symmetric).astype(jnp.float32)


def draw_lower_inverse(key, part):
    key = jax.random.fold_in(key, 23)
    off_key, diag_key = jax.random.split(key)
    off_vals = jax.random.normal(off_key, (B, B), jnp.float32) * (0.075 / B ** 0.5)
    diag_vals = 0.1 + 0.1 * jax.random.uniform(diag_key, (B,), jnp.float32)
    row_ids = jnp.arange(B, dtype=jnp.int32)
    below = row_ids[:, None] > row_ids[None, :]
    on_diag = row_ids[:, None] == row_ids[None, :]
    return jnp.where(on_diag, diag_vals[None, :], jnp.where(below, off_vals, 0.0)).astype(jnp.float32)


def touch_ends(values, own_key, smallest, largest):
    spot = [jax.random.randint(jax.random.fold_in(own_key, axis), (), 0, length) for axis, length in enumerate(values.shape)]
    longest = values.shape.index(max(values.shape))
    neighbour = spot[:longest] + [(spot[longest] + 1) % values.shape[longest]] + spot[longest + 1:]
    return values.at[tuple(spot)].set(smallest).at[tuple(neighbour)].set(largest)


def block_levels(stream_key, dims, cuts, low, high):
    def one(dim, shards_of):
        heights = jax.random.uniform(jax.random.fold_in(jax.random.fold_in(stream_key, 6), dim), (shards_of,), jnp.float32, low / len(cuts), high / len(cuts))
        return jnp.repeat(jnp.exp(heights), dims[dim] // shards_of).reshape((-1,) + (1,) * (len(dims) - dim - 1))

    gain = one(*cuts[0])
    for cut in cuts[1:]:
        gain = gain * one(*cut)
    return gain


def gaussian(own_key, dims, deviation, bound, pieces=(), kind=jnp.bfloat16):
    gain = block_levels(own_key, dims, pieces, -0.22, 0.18) if pieces else 1.0
    array = jax.random.normal(own_key, dims, jnp.float32) * deviation * gain
    return jnp.minimum(jnp.maximum(array, -bound), bound).astype(kind)


def setup_inputs(seed: int = 0) -> dict:
    arg_keys = jax.random.split(jax.random.key(seed), 5)
    matrix = draw_matrix(jax.random.fold_in(arg_keys[4], 71), 0)
    lower_inverse = draw_lower_inverse(jax.random.fold_in(arg_keys[4], 71), 0)
    rhs = gaussian(arg_keys[2], (W, R), 1.0, 6.0, ((0, 32), (1, 16)), jnp.float32)
    sources = touch_ends(jax.random.randint(arg_keys[3], (R,), 0, W), jax.random.fold_in(arg_keys[3], 1), 0, W - 1).astype(jnp.int32)
    return {"matrix": matrix, "lower_inverse": lower_inverse, "rhs": rhs, "sources": sources}


def reference(matrix, lower_inverse, rhs, sources):
    highest = lax.Precision.HIGHEST
    row_ids = jnp.arange(W, dtype=jnp.int32)
    driven = rhs + (row_ids[:, None] == sources[None, :]).astype(jnp.float32)
    factor = jnp.dot(matrix[B:, :B], lower_inverse.T, precision=highest, preferred_element_type=jnp.float32)
    top_solve = jnp.dot(lower_inverse, driven[:B], precision=highest, preferred_element_type=jnp.float32)
    trailing = matrix[B:, B:] - jnp.dot(factor, factor.T, precision=highest, preferred_element_type=jnp.float32)
    updated = matrix.at[B:, B:].set(trailing).at[B:, :B].set(factor)
    remaining = driven[B:] - jnp.dot(factor, top_solve, precision=highest, preferred_element_type=jnp.float32)
    rhs_out = jnp.concatenate([top_solve, remaining], axis=0)
    return updated, rhs_out
```

```python
import functools

import jax
import jax.numpy as jnp
from jax import lax
from jax.experimental import pallas as pl
from jax.experimental.pallas import tpu as pltpu
from jax.sharding import PartitionSpec as P

MESH = pl.DeviceIdType.MESH
NY = 8
NX = 4
NL = 4


def coords():
    r = lax.axis_index("row")
    q = lax.axis_index("col")
    return r // 16, (r // 2) % NY, r % 2, q // NL, q % NL


def device(h, y, c, x, l):
    return (h * 16 + y * 2 + c, x * NL + l)


def remote(src, dst, send, recv, target):
    return pltpu.make_async_remote_copy(
        src_ref=src,
        dst_ref=dst,
        send_sem=send,
        recv_sem=recv,
        device_id=device(*target),
        device_id_type=MESH,
    )


def spread_kernel(
    matrix, rhs_t, left, top,
    t1_send, t_send, s_send, p1_send, p_send,
    t_recv, s_recv, p_recv, local_sem,
):
    h, y, c, x, l = coords()
    s = 1 - 2 * c
    top_root = (h == 0) & (y == 0) & (c == 0)
    left_root = (x == 0) & (l == 0)

    def yy(k):
        return lax.rem(y + k + 2 * NY, NY)

    def xx(k):
        return lax.rem(x + k, NX)

    def ll(k):
        return lax.rem(l + k, NL)

    barrier = pltpu.get_barrier_semaphore()

    def greet(target):
        pl.semaphore_signal(barrier, inc=1, device_id=device(*target), device_id_type=MESH)

    greet((h, y, 1 - c, x, l))
    greet((1 - h, y, c, x, l))
    for k in range(1, NY):
        greet((h, yy(k), c, x, l))
    for k in range(1, NL):
        greet((h, y, c, x, ll(k)))
    for k in range(1, NX):
        greet((h, y, c, xx(k), l))

    @pl.when(top_root)
    def _():
        for k in range(1, NY):
            greet((0, k, 1, x, l))

    far_top = (h == 0) & (y > 0) & (c == 1)

    @pl.when(far_top)
    def _():
        greet((0, 0, 0, x, l))

    @pl.when(left_root)
    def _():
        for a in range(1, NX):
            for b in range(1, NL):
                greet((h, y, c, a, b))

    far_left = (x > 0) & (l > 0)

    @pl.when(far_left)
    def _():
        greet((h, y, c, 0, 0))

    def local_top():
        return (
            pltpu.make_async_copy(
                matrix.at[pl.ds(0, 128), pl.ds(0, 128)], top.at[0, 0, pl.ds(0, 128)], local_sem.at[0]
            ),
            pltpu.make_async_copy(
                rhs_t.at[pl.ds(0, 8), pl.ds(0, 128)], top.at[0, 0, pl.ds(128, 8)], local_sem.at[1]
            ),
        )

    def local_left():
        return pltpu.make_async_copy(
            matrix.at[pl.ds(0, 32), pl.ds(0, 256)], left.at[0, 0], local_sem.at[2]
        )

    @pl.when(top_root)
    def _():
        for copy in local_top():
            copy.start()

    @pl.when(left_root)
    def _():
        local_left().start()

    expected = (
        2 + (NY - 1) + (NL - 1) + (NX - 1)
        + jnp.where(top_root, NY - 1, 0)
        + jnp.where(far_top, 1, 0)
        + jnp.where(left_root, (NX - 1) * (NL - 1), 0)
        + jnp.where(far_left, 1, 0)
    )
    pl.semaphore_wait(barrier, expected)

    top_order = [
        (a, b) for a in (4, 3, 5, 2, 6, 1, 7, 0) for b in (0, 1) if (a, b) != (0, 0)
    ]

    def top_scatter(a, b):
        j = a * 2 + b
        return (
            remote(
                matrix.at[pl.ds(b * 128, 128), pl.ds(a * 128, 128)],
                top.at[a, b, pl.ds(0, 128)],
                t1_send.at[2 * j], t_recv.at[a], (0, a, b, x, l),
            ),
            remote(
                rhs_t.at[pl.ds((a // 2) * 8, 8), pl.ds((a % 2) * 128, 128)],
                top.at[a, b, pl.ds(128, 8)],
                t1_send.at[2 * j + 1], t_recv.at[a], (0, a, b, x, l),
            ),
        )

    left_order = [
        (a, b) for b in (3, 2, 1, 0) for a in (2, 1, 3, 0) if (a, b) != (0, 0)
    ]

    def left_scatter(a, b):
        return remote(
            matrix.at[pl.ds(a * 128 + b * 32, 32), pl.ds(0, 256)],
            left.at[a, b],
            p1_send.at[a * NL + b], p_recv.at[a * NL + b], (h, y, c, a, b),
        )

    @pl.when(left_root)
    def _():
        for a, b in left_order:
            left_scatter(a, b).start()

    @pl.when(top_root)
    def _():
        for a, b in top_order:
            for copy in top_scatter(a, b):
                copy.start()

    def left_copy(a, b, j, target):
        return remote(left.at[a, b], left.at[a, b], p_send.at[j], p_recv.at[a * NL + b], target)

    def left_wait(a, b):
        left_copy(a, b, 0, (h, y, c, x, l)).wait_recv()

    def top_copy(a, j, target):
        return remote(top.at[a, c], top.at[a, c], t_send.at[j], t_recv.at[a], target)

    def top_wait(a):
        top_copy(a, 0, (h, y, c, x, l)).wait_recv()

    def sibling(a, half):
        return remote(
            top.at[a, half], top.at[a, half], s_send.at[a], s_recv.at[a], (h, y, 1 - c, x, l)
        )

    @pl.when(left_root)
    def _():
        local_left().wait()

    @pl.when(jnp.logical_not(left_root))
    def _():
        left_wait(x, l)

    for k in (2, 1, 3):
        left_copy(x, l, k - 1, (h, y, c, x, ll(k))).start()
    for k in (2, 1, 3):
        left_copy(x, l, 2 + k, (h, y, c, xx(k), l)).start()

    def own_top():
        top_copy(y, 0, (h, yy(2), c, x, l)).start()
        top_copy(y, 1, (h, yy(-2), c, x, l)).start()
        top_copy(y, 2, (h, yy(1), c, x, l)).start()
        top_copy(y, 3, (h, yy(-1), c, x, l)).start()
        sibling(y, c).start()

    def across():
        return top_copy(y, 7, (1, y, c, x, l))

    @pl.when(h == 0)
    def _():
        @pl.when(top_root)
        def _():
            for copy in local_top():
                copy.wait()

        @pl.when(jnp.logical_not(top_root))
        def _():
            top_wait(y)

        across().start()
        own_top()

    for m in (1, 3, 2):
        left_wait(x, ll(m))
        for k in (2, 1, 3):
            left_copy(x, ll(m), 3 * m + 2 + k, (h, y, c, xx(k), l)).start()

    @pl.when(h == 1)
    def _():
        top_wait(y)
        own_top()

    top_wait(yy(-2 * s))
    top_copy(yy(-2 * s), 4, (h, yy(2 * s), c, x, l)).start()
    top_copy(yy(-2 * s), 5, (h, yy(s), c, x, l)).start()
    sibling(yy(-2 * s), c).start()
    top_wait(yy(2 * s))
    top_copy(yy(2 * s), 6, (h, yy(-s), c, x, l)).start()
    sibling(yy(2 * s), c).start()
    for k in (1, -1, 3, -3, 4):
        top_wait(yy(k))
        sibling(yy(k), c).start()

    for k in range(1, NX):
        for b in range(NL):
            left_wait(xx(k), b)
    for k in (0, 2, -2, 1, -1, 3, -3, 4):
        a = yy(k)
        remote(
            top.at[a, 1 - c], top.at[a, 1 - c], s_send.at[a], s_recv.at[a], (h, y, 1 - c, x, l)
        ).wait_recv()

    for k in range(15):
        left_copy(x, l, k, (h, y, c, x, l)).wait_send()
    for k in range(7):
        top_copy(y, k, (h, y, c, x, l)).wait_send()
    for a in range(NY):
        sibling(a, c).wait_send()

    @pl.when(h == 0)
    def _():
        across().wait_send()

    @pl.when(left_root)
    def _():
        for a, b in left_order:
            left_scatter(a, b).wait_send()

    @pl.when(top_root)
    def _():
        for a, b in top_order:
            for copy in top_scatter(a, b):
                copy.wait_send()


def spread(matrix, rhs_t):
    dma = pltpu.SemaphoreType.DMA
    return pl.pallas_call(
        spread_kernel,
        out_shape=(
            jax.ShapeDtypeStruct((NX, NL, 32, 256), jnp.float32),
            jax.ShapeDtypeStruct((NY, 2, 136, 128), jnp.float32),
        ),
        in_specs=[pl.BlockSpec(memory_space=pl.ANY)] * 2,
        out_specs=(pl.BlockSpec(memory_space=pltpu.VMEM),) * 2,
        scratch_shapes=[
            dma((32,)), dma((8,)), dma((8,)), dma((16,)), dma((15,)),
            dma((8,)), dma((8,)), dma((16,)), dma((3,)),
        ],
        compiler_params=pltpu.CompilerParams(
            collective_id=0, has_side_effects=True, vmem_limit_bytes=16 << 20
        ),
        name="spread_panel",
    )(matrix, rhs_t)


def halves(value):
    high = value.astype(jnp.bfloat16)
    return high, (value - high.astype(jnp.float32)).astype(jnp.bfloat16)


def dot3(a, b, contract):
    (ah, al), (bh, bl) = a, b

    def one(u, v):
        return lax.dot_general(u, v, (contract, ((), ())), preferred_element_type=jnp.float32)

    return one(ah, bh) + (one(ah, bl) + one(al, bh))


def update_kernel(left, top, matrix, inverse, rhs_t, sources, updated, rhs_out, result, out_sem):
    row_index = lax.axis_index("row")
    col_index = lax.axis_index("col")
    inv = halves(inverse[...])
    nt = ((1,), (1,))
    nn = ((1,), (0,))
    wide = jnp.broadcast_to(sources[...].astype(jnp.float32), (32, 32))
    eye = lax.broadcasted_iota(jnp.int32, (32, 32), 0) == lax.broadcasted_iota(jnp.int32, (32, 32), 1)
    column = jnp.sum(jnp.where(eye, wide, 0.0), axis=1, keepdims=True).astype(jnp.int32)
    ids = lax.broadcasted_iota(jnp.int32, (32, 512), 1)
    driven = rhs_t[...] + jnp.where(ids + row_index * 512 == column, 1.0, 0.0)
    top_rhs = jnp.concatenate(
        [
            jnp.concatenate([top[2 * i, 0, pl.ds(128, 8), :], top[2 * i + 1, 0, pl.ds(128, 8), :]], axis=1)
            for i in range(4)
        ],
        axis=0,
    )
    top_driven = top_rhs + jnp.where(
        lax.broadcasted_iota(jnp.int32, (32, 256), 1) == column, 1.0, 0.0
    )
    solve = dot3(halves(top_driven), inv, nt)
    solve_halves = halves(solve)
    panel = jnp.concatenate(
        [jnp.concatenate([top[i, b, pl.ds(0, 128), :] for i in range(NY)], axis=1) for b in range(2)],
        axis=0,
    )
    wide_factor = halves(dot3(inv, halves(panel), nn))
    copies = []
    for i in range(NX):
        rows = pl.ds(i * 128, 128)
        block = jnp.concatenate([left[i, b] for b in range(NL)], axis=0)
        factor = dot3(halves(block), inv, nt)
        factor_halves = halves(factor)
        product = dot3(factor_halves, wide_factor, nn)
        held = matrix[rows, :]
        result[rows, :] = held - product

        @pl.when(col_index == 0)
        def _():
            result[rows, pl.ds(0, 256)] = factor

        if i < 2:
            @pl.when(row_index == 0)
            def _():
                result[rows, :] = held

        copy = pltpu.make_async_copy(result.at[rows], updated.at[rows], out_sem.at[i])
        copy.start()
        copies.append(copy)
        rest = driven[:, i * 128:(i + 1) * 128] - dot3(solve_halves, factor_halves, nt)
        if i < 2:
            rest = jnp.where(row_index == 0, solve[:, i * 128:(i + 1) * 128], rest)
        rhs_out[:, pl.ds(i * 128, 128)] = rest
    for copy in copies:
        copy.wait()


def update(left, top, matrix, inverse, rhs_t, sources):
    vmem = pl.BlockSpec(memory_space=pltpu.VMEM)
    return pl.pallas_call(
        update_kernel,
        out_shape=(
            jax.ShapeDtypeStruct((512, 1024), jnp.float32),
            jax.ShapeDtypeStruct((32, 512), jnp.float32),
        ),
        in_specs=[vmem] * 6,
        out_specs=(pl.BlockSpec(memory_space=pl.ANY), vmem),
        scratch_shapes=[pltpu.VMEM((512, 1024), jnp.float32), pltpu.SemaphoreType.DMA((NX,))],
        compiler_params=pltpu.CompilerParams(vmem_limit_bytes=24 << 20),
        name="update_trailing",
    )(left, top, matrix, inverse, rhs_t, sources)


def shards(matrix, lower_inverse, rhs, sources):
    rhs_t = rhs.T
    left, top = spread(matrix, rhs_t)
    updated, rhs_out = update(left, top, matrix, lower_inverse, rhs_t, sources.reshape(1, -1))
    return updated, rhs_out.T


def solution(mesh):
    placed = (P("row", "col"), P(), P("row", "col"), P("col"))
    return jax.shard_map(
        shards,
        mesh=mesh,
        in_specs=placed,
        out_specs=(P("row", "col"), P("row", "col")),
        check_vma=False,
    )
```

```python
import functools

import jax
import jax.numpy as jnp
from jax import lax
from jax.experimental import pallas as pl
from jax.experimental.pallas import tpu as pltpu
from jax.sharding import PartitionSpec as P

MESH = pl.DeviceIdType.MESH
NY = 8
NX = 4
NL = 4
NT = ((1,), (1,))
NN = ((1,), (0,))


def coords():
    r = lax.axis_index("row")
    q = lax.axis_index("col")
    return r // 16, (r // 2) % NY, r % 2, q // NL, q % NL


def device(h, y, c, x, l):
    return (h * 16 + y * 2 + c, x * NL + l)


def remote(src, dst, send, recv, target):
    return pltpu.make_async_remote_copy(
        src_ref=src,
        dst_ref=dst,
        send_sem=send,
        recv_sem=recv,
        device_id=device(*target),
        device_id_type=MESH,
    )


def halves(value):
    high = value.astype(jnp.bfloat16)
    return high, (value - high.astype(jnp.float32)).astype(jnp.bfloat16)


def dot3(a, b, contract):
    (ah, al), (bh, bl) = a, b

    def one(u, v):
        return lax.dot_general(u, v, (contract, ((), ())), preferred_element_type=jnp.float32)

    return one(ah, bh) + (one(ah, bl) + one(al, bh))


def spread_kernel(
    matrix, rhs_t, inverse,
    factor, factor_hi, factor_lo, wide_hi, wide_lo, inv_hi, inv_lo, top_rhs,
    left, top, inv,
    t1_send, t_send, s_send, p1_send, p_send,
    t_recv, s_recv, p_recv, local_sem, ready, ready_top, ready_left,
):
    h, y, c, x, l = coords()
    s = 1 - 2 * c
    top_root = (h == 0) & (y == 0) & (c == 0)
    left_root = (x == 0) & (l == 0)
    no = jnp.logical_not
    on = pl.when

    def yy(k):
        return lax.rem(y + k + 2 * NY, NY)

    def xx(k):
        return lax.rem(x + k, NX)

    def ll(k):
        return lax.rem(l + k, NL)

    load_inverse = pltpu.make_async_copy(inverse, inv, local_sem.at[0])
    load_left = pltpu.make_async_copy(matrix.at[:, pl.ds(0, 256)], left, local_sem.at[1])

    @on(top_root)
    def _():
        for a in range(NY):
            for b in range(2):
                pltpu.make_async_copy(
                    matrix.at[pl.ds(b * 128, 128), pl.ds(a * 128, 128)],
                    top.at[a, b, pl.ds(0, 128)], local_sem.at[2],
                ).start()
                pltpu.make_async_copy(
                    rhs_t.at[pl.ds((a // 2) * 8, 8), pl.ds((a % 2) * 128, 128)],
                    top.at[a, b, pl.ds(128, 8)], local_sem.at[2],
                ).start()

    @on(left_root)
    def _():
        load_left.start()

    load_inverse.start()

    barrier = pltpu.get_barrier_semaphore()

    def signal(semaphore, target):
        pl.semaphore_signal(semaphore, inc=1, device_id=device(*target), device_id_type=MESH)

    def rank(v, n):
        return jnp.minimum(v, n - v) * n + v

    partners = []
    for k, slot, back in ((2, 2, 3), (-2, 3, 2), (1, 0, 1), (-1, 1, 0)):
        partners.append((slot, back, (h, yy(k), c, x, l), rank(y, NY) < rank(yy(k), NY)))
    partners.append((10, 10, (1 - h, y, c, x, l), h == 0))
    for k, slot, back in ((2, 8, 8), (1, 7, 9), (3, 9, 7)):
        partners.append((slot, back, (h, y, c, x, ll(k)), l < ll(k)))
    for k, slot, back in ((2, 5, 5), (1, 4, 6), (3, 6, 4)):
        partners.append((slot, back, (h, y, c, xx(k), l), rank(x, NX) < rank(xx(k), NX)))
    partners.append((11, 11, (h, y, 1 - c, x, l), c == 0))
    earlier = {slot: early for slot, _, _, early in partners}

    near = jnp.minimum(y, NY - y)
    far_top = (h == 0) & (((c == 1) & (y > 0)) | ((c == 0) & (near > 2)))
    far_left = (x > 0) & (l > 0)

    @on(top_root)
    def _():
        for a in (1, 7, 2, 6, 3, 5, 4):
            signal(barrier, (0, a, 1, x, l))
        for a in (3, 5, 4):
            signal(barrier, (0, a, 0, x, l))

    @on(left_root)
    def _():
        for a in range(1, NX):
            for b in range(1, NL):
                signal(barrier, (h, y, c, a, b))

    expected = jnp.where(far_top, 1, 0) + jnp.where(far_left, 1, 0)
    for slot, back, target, early in partners:
        expected = expected + jnp.where(early, 0, 1)

        @on(early)
        def _():
            signal(barrier, target)

    @on(expected > 0)
    def _():
        pl.semaphore_wait(barrier, expected)

    @on(far_top)
    def _():
        signal(ready_top.at[y], (0, 0, 0, x, l))

    @on(far_left)
    def _():
        signal(ready_left.at[x * NL + l], (h, y, c, 0, 0))

    for slot, back, target, early in partners:
        @on(no(early))
        def _():
            signal(ready.at[back], target)

    def need(slot):
        @on(earlier[slot])
        def _():
            pl.semaphore_wait(ready.at[slot], 1)

    def piece(a, b):
        return left.at[pl.ds(pl.multiple_of(a * 128 + b * 32, 32), 32)]

    def left_scatter(a, b):
        return remote(
            piece(a, b), piece(a, b), p1_send.at[a * NL + b], p_recv.at[a * NL + b], (h, y, c, a, b)
        )

    def left_copy(a, b, j, target):
        return remote(piece(a, b), piece(a, b), p_send.at[j], p_recv.at[a * NL + b], target)

    def left_wait(a, b):
        @on(no(left_root))
        def _():
            left_copy(a, b, 0, (h, y, c, x, l)).wait_recv()

    def top_scatter(a, b):
        return remote(
            top.at[a, b], top.at[a, b], t1_send.at[a * 2 + b], t_recv.at[a], (0, a, b, x, l)
        )

    def top_beside(a):
        return remote(
            top.at[a, 1], top.at[a, 1], t1_send.at[16 + a], t_recv.at[a], (0, 0, 1, x, l)
        )

    def top_copy(a, j, target):
        return remote(top.at[a, c], top.at[a, c], t_send.at[j], t_recv.at[a], target)

    def top_wait(a):
        @on(no(top_root))
        def _():
            top_copy(a, 0, (h, y, c, x, l)).wait_recv()

    def has_all(k):
        return (h == 0) & (yy(k) == 0)

    def top_send(a, j, k):
        @on(no(has_all(k)))
        def _():
            top_copy(a, j, (h, yy(k), c, x, l)).start()

    def sibling(a, half):
        return remote(
            top.at[a, half], top.at[a, half], s_send.at[a], s_recv.at[a], (h, y, 1 - c, x, l)
        )

    beside_root = (h == 0) & (y == 0) & (c == 1)

    def sibling_send(a):
        @on(no(beside_root))
        def _():
            sibling(a, c).start()

    def top_pair(a, slot):
        if slot is None:
            pl.semaphore_wait(ready_top.at[a], 2)
        else:
            need(slot)
            pl.semaphore_wait(ready_top.at[a], 1)
        for b in range(2):
            top_scatter(a, b).start()

    @on(top_root)
    def _():
        pltpu.make_async_copy(top, top, local_sem.at[2]).wait()
        top_pair(1, 0)
        top_pair(7, 1)
        top_pair(2, 2)
        top_pair(6, 3)

    left_order = [
        (1, 0), (3, 0), (0, 1), (2, 0), (1, 1), (3, 1), (0, 2), (2, 1),
        (1, 2), (3, 2), (0, 3), (2, 2), (1, 3), (3, 3), (2, 3),
    ]

    @on(left_root)
    def _():
        load_left.wait()
        for a, b in left_order:
            if b == 0:
                need({1: 4, 2: 5, 3: 6}[a])
            elif a == 0:
                need({1: 7, 2: 8, 3: 9}[b])
            else:
                pl.semaphore_wait(ready_left.at[a * NL + b], 1)
            left_scatter(a, b).start()

    @on(top_root)
    def _():
        top_pair(3, None)
        top_pair(5, None)
        top_pair(4, None)
        need(11)
        top_scatter(0, 1).start()
        for a in (6, 2, 1, 7, 3, 5, 4):
            top_beside(a).start()

    load_inverse.wait()
    high, low = halves(inv[...])
    inv_hi[...] = high
    inv_lo[...] = low

    def own_left():
        left_wait(x, l)

        @on(no(left_root))
        def _():
            for slot in (8, 7, 9, 5, 4, 6):
                need(slot)

        for k in (2, 1, 3):
            @on(no((x == 0) & (ll(k) == 0)))
            def _():
                left_copy(x, l, k - 1, (h, y, c, x, ll(k))).start()
        for k in (2, 1, 3):
            @on(no((l == 0) & (xx(k) == 0)))
            def _():
                left_copy(x, l, 2 + k, (h, y, c, xx(k), l)).start()

    def own_top():
        top_wait(y)

        @on(no(top_root))
        def _():
            for slot in (2, 3, 0, 1, 11):
                need(slot)

        for k in (2, -2, 1, -1):
            top_send(y, 3 + k, k)

        @on(h == 0)
        def _():
            need(10)
            top_copy(y, 10, (1, y, c, x, l)).start()

        sibling_send(y)

    def left_relay():
        for m in (1, 3, 2):
            left_wait(x, ll(m))
            for k in (2, 1, 3):
                @on(no((l == 0) & (xx(k) == 0)))
                def _():
                    left_copy(x, ll(m), 3 * m + 2 + k, (h, y, c, xx(k), l)).start()

    ahead = yy(-2 * s)
    behind = yy(2 * s)

    def top_relay():
        top_wait(ahead)
        top_send(ahead, 3, 2 * s)
        top_send(ahead, 8, s)
        sibling_send(ahead)
        top_wait(behind)
        top_send(behind, 9, -s)
        sibling_send(behind)

    def top_tail(k):
        top_wait(yy(k))
        sibling_send(yy(k))

    inv_halves = (inv_hi[...], inv_lo[...])

    def narrow(i):
        rows = pl.ds(i * 128, 128)
        part = dot3(halves(left[rows, :]), inv_halves, NT)
        factor[rows, :] = part
        high, low = halves(part)
        factor_hi[rows, :] = high
        factor_lo[rows, :] = low

    def broad(k):
        a = yy(k)

        @on(no(top_root))
        def _():
            sibling(a, 1 - c).wait_recv()

        chunk = jnp.concatenate([top[a, b, pl.ds(0, 128), :] for b in range(2)], axis=0)
        high, low = halves(dot3(inv_halves, halves(chunk), NN))
        wide_hi[a] = high
        wide_lo[a] = low
        top_rhs[a] = top[a, 0, pl.ds(128, 8), :]

    @on(h == 0)
    def _():
        own_top()
        own_left()
        top_relay()
        left_relay()

    @on(h == 1)
    def _():
        own_left()
        left_relay()
        own_top()
        top_relay()

    for k in (1, -1):
        top_tail(k)
    for b in range(NL):
        for k in (1, 3, 2):
            left_wait(xx(k), b)
    narrow(0)
    narrow(1)
    top_tail(3)
    narrow(2)
    top_tail(-3)
    narrow(3)
    broad(0)
    top_tail(4)
    for k in (2, -2, 1, -1, 3, -3, 4):
        broad(k)

    for k in (1, 2, 3):
        @on(no((x == 0) & (ll(k) == 0)))
        def _():
            left_copy(x, l, k - 1, (h, y, c, x, l)).wait_send()

        @on(no((l == 0) & (xx(k) == 0)))
        def _():
            for m in range(NL):
                left_copy(x, l, 3 * m + 2 + k, (h, y, c, x, l)).wait_send()

    for j, k in ((1, -2), (2, -1), (4, 1), (5, 2), (3, 2 * s), (8, s), (9, -s)):
        @on(no(has_all(k)))
        def _():
            top_copy(y, j, (h, y, c, x, l)).wait_send()

    @on(no(beside_root))
    def _():
        for a in range(NY):
            sibling(a, c).wait_send()

    @on(h == 0)
    def _():
        top_copy(y, 10, (h, y, c, x, l)).wait_send()

    @on(left_root)
    def _():
        for a, b in left_order:
            left_scatter(a, b).wait_send()

    @on(top_root)
    def _():
        top_scatter(0, 1).wait_send()
        for a in range(1, NY):
            top_beside(a).wait_send()
            for b in range(2):
                top_scatter(a, b).wait_send()


def spread(matrix, rhs_t, inverse, sources=None):
    hbm = lambda value: pltpu.with_memory_space_constraint(value, pltpu.HBM)
    dma = pltpu.SemaphoreType.DMA
    regular = pltpu.SemaphoreType.REGULAR
    f32 = jnp.float32
    b16 = jnp.bfloat16
    return pl.pallas_call(
        spread_kernel,
        out_shape=(
            jax.ShapeDtypeStruct((512, 256), f32),
            jax.ShapeDtypeStruct((512, 256), b16),
            jax.ShapeDtypeStruct((512, 256), b16),
            jax.ShapeDtypeStruct((NY, 256, 128), b16),
            jax.ShapeDtypeStruct((NY, 256, 128), b16),
            jax.ShapeDtypeStruct((256, 256), b16),
            jax.ShapeDtypeStruct((256, 256), b16),
            jax.ShapeDtypeStruct((NY, 8, 128), f32),
        ),
        in_specs=[pl.BlockSpec(memory_space=pltpu.HBM)] * 3,
        out_specs=(pl.BlockSpec(memory_space=pltpu.VMEM),) * 8,
        scratch_shapes=[
            pltpu.VMEM((512, 256), f32),
            pltpu.VMEM((NY, 2, 136, 128), f32),
            pltpu.VMEM((256, 256), f32),
            dma((24,)), dma((11,)), dma((8,)), dma((16,)), dma((15,)),
            dma((8,)), dma((8,)), dma((16,)), dma((3,)),
            regular((12,)), regular((8,)), regular((16,)),
        ],
        compiler_params=pltpu.CompilerParams(
            collective_id=0, has_side_effects=True, vmem_limit_bytes=24 << 20
        ),
        name="spread_panel",
    )(hbm(matrix), hbm(rhs_t), hbm(inverse))


def update_kernel(
    factor, factor_hi, factor_lo, wide_hi, wide_lo, inv_hi, inv_lo, top_rhs,
    matrix, rhs_t, sources, updated, rhs_out, result, out_sem,
):
    row_index = lax.axis_index("row")
    col_index = lax.axis_index("col")
    wide = tuple(
        jnp.concatenate([ref[i] for i in range(NY)], axis=1) for ref in (wide_hi, wide_lo)
    )
    copies = []
    for i in range(NX):
        rows = pl.ds(i * 128, 128)
        product = dot3((factor_hi[rows, :], factor_lo[rows, :]), wide, NN)
        held = matrix[rows, :]
        result[rows, :] = held - product

        @pl.when(col_index == 0)
        def _():
            result[rows, pl.ds(0, 256)] = factor[rows, :]

        if i < 2:
            @pl.when(row_index == 0)
            def _():
                result[rows, :] = held

        copy = pltpu.make_async_copy(result.at[rows], updated.at[rows], out_sem.at[i])
        copy.start()
        copies.append(copy)

    spare = jnp.broadcast_to(sources[...].astype(jnp.float32), (32, 32))
    eye = lax.broadcasted_iota(jnp.int32, (32, 32), 0) == lax.broadcasted_iota(jnp.int32, (32, 32), 1)
    column = jnp.sum(jnp.where(eye, spare, 0.0), axis=1, keepdims=True).astype(jnp.int32)
    ids = lax.broadcasted_iota(jnp.int32, (32, 512), 1)
    driven = rhs_t[...] + jnp.where(ids + row_index * 512 == column, 1.0, 0.0)
    first = jnp.concatenate(
        [jnp.concatenate([top_rhs[2 * i], top_rhs[2 * i + 1]], axis=1) for i in range(4)], axis=0
    )
    first = first + jnp.where(ids[:, :256] == column, 1.0, 0.0)
    solve = dot3(halves(first), (inv_hi[...], inv_lo[...]), NT)
    rest = driven - dot3(halves(solve), (factor_hi[...], factor_lo[...]), NT)
    rhs_out[...] = rest

    @pl.when(row_index == 0)
    def _():
        rhs_out[:, pl.ds(0, 256)] = solve

    for copy in copies:
        copy.wait()


def update(parts, matrix, rhs_t, sources):
    vmem = pl.BlockSpec(memory_space=pltpu.VMEM)
    return pl.pallas_call(
        update_kernel,
        out_shape=(
            jax.ShapeDtypeStruct((512, 1024), jnp.float32),
            jax.ShapeDtypeStruct((32, 512), jnp.float32),
        ),
        in_specs=[vmem] * 11,
        out_specs=(pl.BlockSpec(memory_space=pl.ANY), vmem),
        scratch_shapes=[pltpu.VMEM((512, 1024), jnp.float32), pltpu.SemaphoreType.DMA((NX,))],
        compiler_params=pltpu.CompilerParams(vmem_limit_bytes=24 << 20),
        name="update_trailing",
    )(*parts, matrix, rhs_t, sources)


def shards(matrix, lower_inverse, rhs, sources):
    rhs_t = rhs.T
    parts = spread(matrix, rhs_t, lower_inverse)
    updated, rhs_out = update(parts, matrix, rhs_t, sources.reshape(1, -1))
    return updated, rhs_out.T


def solution(mesh):
    placed = (P("row", "col"), P(), P("row", "col"), P("col"))
    return jax.shard_map(
        shards,
        mesh=mesh,
        in_specs=placed,
        out_specs=(P("row", "col"), P("row", "col")),
        check_vma=False,
    )
```

```python
import functools

import jax
import jax.numpy as jnp
from jax import lax
from jax.experimental import pallas as pl
from jax.experimental.pallas import tpu as pltpu
from jax.sharding import PartitionSpec as P

MESH = pl.DeviceIdType.MESH
NY = 8
NX = 4
NL = 4
NT = ((1,), (1,))
NN = ((1,), (0,))


def coords():
    r = lax.axis_index("row")
    q = lax.axis_index("col")
    return r // 16, (r // 2) % NY, r % 2, q // NL, q % NL


def device(h, y, c, x, l):
    return (h * 16 + y * 2 + c, x * NL + l)


def remote(src, dst, send, recv, target):
    return pltpu.make_async_remote_copy(
        src_ref=src,
        dst_ref=dst,
        send_sem=send,
        recv_sem=recv,
        device_id=device(*target),
        device_id_type=MESH,
    )


def halves(value):
    high = value.astype(jnp.bfloat16)
    return high, (value - high.astype(jnp.float32)).astype(jnp.bfloat16)


def dot3(a, b, contract):
    (ah, al), (bh, bl) = a, b

    def one(u, v):
        return lax.dot_general(u, v, (contract, ((), ())), preferred_element_type=jnp.float32)

    return one(ah, bh) + (one(ah, bl) + one(al, bh))


def spread_kernel(
    matrix, rhs_t, inverse,
    factor, factor_hi, factor_lo, wide_hi, wide_lo, inv_hi, inv_lo, top_rhs,
    left, top, inv,
    t1_send, t_send, s_send, p1_send, p_send,
    t_recv, s_recv, p_recv, local_sem, ready, ready_top, ready_left,
):
    h, y, c, x, l = coords()
    s = 1 - 2 * c
    top_root = (h == 0) & (y == 0) & (c == 0)
    left_root = (x == 0) & (l == 0)
    no = jnp.logical_not
    on = pl.when

    def yy(k):
        return lax.rem(y + k + 2 * NY, NY)

    def xx(k):
        return lax.rem(x + k, NX)

    def ll(k):
        return lax.rem(l + k, NL)

    load_inverse = pltpu.make_async_copy(inverse, inv, local_sem.at[0])
    load_left = pltpu.make_async_copy(matrix.at[:, pl.ds(0, 256)], left, local_sem.at[1])

    @on(top_root)
    def _():
        for a in range(NY):
            for b in range(2):
                pltpu.make_async_copy(
                    matrix.at[pl.ds(b * 128, 128), pl.ds(a * 128, 128)],
                    top.at[a, b, pl.ds(0, 128)], local_sem.at[2],
                ).start()
                pltpu.make_async_copy(
                    rhs_t.at[pl.ds((a // 2) * 8, 8), pl.ds((a % 2) * 128, 128)],
                    top.at[a, b, pl.ds(128, 8)], local_sem.at[2],
                ).start()

    @on(left_root)
    def _():
        load_left.start()

    load_inverse.start()

    barrier = pltpu.get_barrier_semaphore()

    def signal(semaphore, target):
        pl.semaphore_signal(semaphore, inc=1, device_id=device(*target), device_id_type=MESH)

    def rank(v, n):
        return jnp.minimum(v, n - v) * n + v

    partners = []
    for k, slot, back in ((2, 2, 3), (-2, 3, 2), (1, 0, 1), (-1, 1, 0)):
        partners.append((slot, back, (h, yy(k), c, x, l), rank(y, NY) < rank(yy(k), NY)))
    partners.append((10, 10, (1 - h, y, c, x, l), h == 0))
    for k, slot, back in ((2, 8, 8), (1, 7, 9), (3, 9, 7)):
        partners.append((slot, back, (h, y, c, x, ll(k)), l < ll(k)))
    for k, slot, back in ((2, 5, 5), (1, 4, 6), (3, 6, 4)):
        partners.append((slot, back, (h, y, c, xx(k), l), rank(x, NX) < rank(xx(k), NX)))
    partners.append((11, 11, (h, y, 1 - c, x, l), c == 0))
    def is_last(target):
        return sum(target) == 0

    last = is_last((h, y, c, x, l))
    partners = [
        (slot, back, target, no(last) & (early | is_last(target)) if slot in (0, 1, 2, 3, 11) else early)
        for slot, back, target, early in partners
    ]
    earlier = {slot: early for slot, _, _, early in partners}

    near = jnp.minimum(y, NY - y)
    far_top = (h == 0) & (((c == 1) & (y > 0)) | ((c == 0) & (near > 2)))
    far_left = (x > 0) & (l > 0)

    top_last = is_last((0, 0, 0, x, l))

    @on(far_top & top_last)
    def _():
        signal(barrier, (0, 0, 0, x, l))

    @on(top_root & no(last))
    def _():
        for a in (1, 7, 2, 6, 3, 5, 4):
            signal(barrier, (0, a, 1, x, l))
        for a in (3, 5, 4):
            signal(barrier, (0, a, 0, x, l))

    @on(left_root)
    def _():
        for a in range(1, NX):
            for b in range(1, NL):
                signal(barrier, (h, y, c, a, b))

    expected = (
        jnp.where(far_top & no(top_last), 1, 0)
        + jnp.where(far_left, 1, 0)
        + jnp.where(last, 10, 0)
    )
    for slot, back, target, early in partners:
        expected = expected + jnp.where(early, 0, 1)

        @on(early)
        def _():
            signal(barrier, target)

    def settle(who):
        @on(who & (expected > 0))
        def _():
            pl.semaphore_wait(barrier, expected)

        @on(who & far_top & no(top_last))
        def _():
            signal(ready_top.at[y], (0, 0, 0, x, l))

        @on(who & far_left)
        def _():
            signal(ready_left.at[x * NL + l], (h, y, c, 0, 0))

        for slot, back, target, early in partners:
            @on(who & no(early))
            def _():
                signal(ready.at[back], target)

    first_root = top_root & no(last)
    settle(no(first_root))

    def need(slot):
        @on(earlier[slot])
        def _():
            pl.semaphore_wait(ready.at[slot], 1)

    def piece(a, b):
        return left.at[pl.ds(pl.multiple_of(a * 128 + b * 32, 32), 32)]

    def left_scatter(a, b):
        return remote(
            piece(a, b), piece(a, b), p1_send.at[a * NL + b], p_recv.at[a * NL + b], (h, y, c, a, b)
        )

    def left_copy(a, b, j, target):
        return remote(piece(a, b), piece(a, b), p_send.at[j], p_recv.at[a * NL + b], target)

    def left_wait(a, b):
        @on(no(left_root))
        def _():
            left_copy(a, b, 0, (h, y, c, x, l)).wait_recv()

    def top_scatter(a, b):
        return remote(
            top.at[a, b], top.at[a, b], t1_send.at[a * 2 + b], t_recv.at[a], (0, a, b, x, l)
        )

    def top_beside(a):
        return remote(
            top.at[a, 1], top.at[a, 1], t1_send.at[16 + a], t_recv.at[a], (0, 0, 1, x, l)
        )

    def top_copy(a, j, target):
        return remote(top.at[a, c], top.at[a, c], t_send.at[j], t_recv.at[a], target)

    def top_wait(a):
        @on(no(top_root))
        def _():
            top_copy(a, 0, (h, y, c, x, l)).wait_recv()

    def has_all(k):
        return (h == 0) & (yy(k) == 0)

    def top_send(a, j, k):
        @on(no(has_all(k)))
        def _():
            top_copy(a, j, (h, yy(k), c, x, l)).start()

    def sibling(a, half):
        return remote(
            top.at[a, half], top.at[a, half], s_send.at[a], s_recv.at[a], (h, y, 1 - c, x, l)
        )

    beside_root = (h == 0) & (y == 0) & (c == 1)

    def sibling_send(a):
        @on(no(beside_root))
        def _():
            sibling(a, c).start()

    def top_pair(a, slot):
        if slot is not None:
            need(slot)

        @on(no(last))
        def _():
            pl.semaphore_wait(ready_top.at[a], 2 if slot is None else 1)

        for b in range(2):
            top_scatter(a, b).start()

    left_order = [
        (1, 0), (3, 0), (0, 1), (2, 0), (1, 1), (3, 1), (0, 2), (2, 1),
        (1, 2), (3, 2), (0, 3), (2, 2), (1, 3), (3, 3), (2, 3),
    ]

    @on(top_root)
    def _():
        pltpu.make_async_copy(top, top, local_sem.at[2]).wait()
        top_pair(1, 0)
        top_pair(7, 1)
        top_pair(2, 2)
        top_pair(6, 3)
        top_pair(3, None)
        top_pair(5, None)
        top_pair(4, None)
        need(11)
        top_scatter(0, 1).start()
        for a in (6, 2, 1, 7, 3, 5, 4):
            top_beside(a).start()

    settle(first_root)

    @on(left_root)
    def _():
        load_left.wait()
        for a, b in left_order:
            if b == 0:
                need({1: 4, 2: 5, 3: 6}[a])
            elif a == 0:
                need({1: 7, 2: 8, 3: 9}[b])
            else:
                pl.semaphore_wait(ready_left.at[a * NL + b], 1)
            left_scatter(a, b).start()

    load_inverse.wait()
    high, low = halves(inv[...])
    inv_hi[...] = high
    inv_lo[...] = low

    def own_left():
        left_wait(x, l)

        @on(no(left_root))
        def _():
            for slot in (8, 7, 9, 5, 4, 6):
                need(slot)

        for k in (2, 1, 3):
            @on(no((x == 0) & (ll(k) == 0)))
            def _():
                left_copy(x, l, k - 1, (h, y, c, x, ll(k))).start()
        for k in (2, 1, 3):
            @on(no((l == 0) & (xx(k) == 0)))
            def _():
                left_copy(x, l, 2 + k, (h, y, c, xx(k), l)).start()

    def own_top():
        top_wait(y)

        @on(no(top_root))
        def _():
            for slot in (2, 3, 0, 1, 11):
                need(slot)

        for k in (2, -2, 1, -1):
            top_send(y, 3 + k, k)

        @on(h == 0)
        def _():
            need(10)
            top_copy(y, 10, (1, y, c, x, l)).start()

        sibling_send(y)

    def left_relay():
        for m in (1, 3, 2):
            left_wait(x, ll(m))
            for k in (2, 1, 3):
                @on(no((l == 0) & (xx(k) == 0)))
                def _():
                    left_copy(x, ll(m), 3 * m + 2 + k, (h, y, c, xx(k), l)).start()

    ahead = yy(-2 * s)
    behind = yy(2 * s)

    def top_relay():
        top_wait(ahead)
        top_send(ahead, 3, 2 * s)
        top_send(ahead, 8, s)
        sibling_send(ahead)
        top_wait(behind)
        top_send(behind, 9, -s)
        sibling_send(behind)

    def top_tail(k):
        top_wait(yy(k))
        sibling_send(yy(k))

    inv_halves = (inv_hi[...], inv_lo[...])

    def block(i):
        rows = pl.ds(pl.multiple_of(i * 128, 128), 128)
        part = dot3(halves(left[rows, :]), inv_halves, NT)
        factor[rows, :] = part
        high, low = halves(part)
        factor_hi[rows, :] = high
        factor_lo[rows, :] = low

    def others(k):
        for b in range(NL):
            left_wait(xx(k), b)
        block(xx(k))

    def broad(k):
        a = yy(k)

        @on(no(top_root))
        def _():
            sibling(a, 1 - c).wait_recv()

        chunk = jnp.concatenate([top[a, b, pl.ds(0, 128), :] for b in range(2)], axis=0)
        high, low = halves(dot3(inv_halves, halves(chunk), NN))
        wide_hi[a] = high
        wide_lo[a] = low
        top_rhs[a] = top[a, 0, pl.ds(128, 8), :]

    @on(h == 0)
    def _():
        own_top()
        own_left()

    @on(h == 1)
    def _():
        own_left()
        own_top()

    left_relay()
    top_relay()
    block(x)
    top_tail(1)
    top_tail(-1)
    others(1)
    top_tail(3)
    others(3)
    top_tail(-3)
    others(2)
    broad(0)
    top_tail(4)
    for k in (2, -2, 1, -1, 3, -3, 4):
        broad(k)

    for k in (1, 2, 3):
        @on(no((x == 0) & (ll(k) == 0)))
        def _():
            left_copy(x, l, k - 1, (h, y, c, x, l)).wait_send()

        @on(no((l == 0) & (xx(k) == 0)))
        def _():
            for m in range(NL):
                left_copy(x, l, 3 * m + 2 + k, (h, y, c, x, l)).wait_send()

    for j, k in ((1, -2), (2, -1), (4, 1), (5, 2), (3, 2 * s), (8, s), (9, -s)):
        @on(no(has_all(k)))
        def _():
            top_copy(y, j, (h, y, c, x, l)).wait_send()

    @on(no(beside_root))
    def _():
        for a in range(NY):
            sibling(a, c).wait_send()

    @on(h == 0)
    def _():
        top_copy(y, 10, (h, y, c, x, l)).wait_send()

    @on(left_root)
    def _():
        for a, b in left_order:
            left_scatter(a, b).wait_send()

    @on(top_root)
    def _():
        top_scatter(0, 1).wait_send()
        for a in range(1, NY):
            top_beside(a).wait_send()
            for b in range(2):
                top_scatter(a, b).wait_send()


def spread(matrix, rhs_t, inverse, sources=None):
    hbm = lambda value: pltpu.with_memory_space_constraint(value, pltpu.HBM)
    dma = pltpu.SemaphoreType.DMA
    regular = pltpu.SemaphoreType.REGULAR
    f32 = jnp.float32
    b16 = jnp.bfloat16
    return pl.pallas_call(
        spread_kernel,
        out_shape=(
            jax.ShapeDtypeStruct((512, 256), f32),
            jax.ShapeDtypeStruct((512, 256), b16),
            jax.ShapeDtypeStruct((512, 256), b16),
            jax.ShapeDtypeStruct((NY, 256, 128), b16),
            jax.ShapeDtypeStruct((NY, 256, 128), b16),
            jax.ShapeDtypeStruct((256, 256), b16),
            jax.ShapeDtypeStruct((256, 256), b16),
            jax.ShapeDtypeStruct((NY, 8, 128), f32),
        ),
        in_specs=[pl.BlockSpec(memory_space=pltpu.HBM)] * 3,
        out_specs=(pl.BlockSpec(memory_space=pltpu.VMEM),) * 8,
        scratch_shapes=[
            pltpu.VMEM((512, 256), f32),
            pltpu.VMEM((NY, 2, 136, 128), f32),
            pltpu.VMEM((256, 256), f32),
            dma((24,)), dma((11,)), dma((8,)), dma((16,)), dma((15,)),
            dma((8,)), dma((8,)), dma((16,)), dma((3,)),
            regular((12,)), regular((8,)), regular((16,)),
        ],
        compiler_params=pltpu.CompilerParams(
            collective_id=0, has_side_effects=True, vmem_limit_bytes=24 << 20
        ),
        name="spread_panel",
    )(hbm(matrix), hbm(rhs_t), hbm(inverse))


def update_kernel(
    factor, factor_hi, factor_lo, wide_hi, wide_lo, inv_hi, inv_lo, top_rhs,
    matrix, rhs_t, sources, updated, rhs_out, result, out_sem,
):
    row_index = lax.axis_index("row")
    col_index = lax.axis_index("col")
    wide = tuple(
        jnp.concatenate([ref[i] for i in range(NY)], axis=1) for ref in (wide_hi, wide_lo)
    )
    copies = []
    for i in range(NX):
        rows = pl.ds(i * 128, 128)
        product = dot3((factor_hi[rows, :], factor_lo[rows, :]), wide, NN)
        held = matrix[rows, :]
        result[rows, :] = held - product

        @pl.when(col_index == 0)
        def _():
            result[rows, pl.ds(0, 256)] = factor[rows, :]

        if i < 2:
            @pl.when(row_index == 0)
            def _():
                result[rows, :] = held

        copy = pltpu.make_async_copy(result.at[rows], updated.at[rows], out_sem.at[i])
        copy.start()
        copies.append(copy)

    spare = jnp.broadcast_to(sources[...].astype(jnp.float32), (32, 32))
    eye = lax.broadcasted_iota(jnp.int32, (32, 32), 0) == lax.broadcasted_iota(jnp.int32, (32, 32), 1)
    column = jnp.sum(jnp.where(eye, spare, 0.0), axis=1, keepdims=True).astype(jnp.int32)
    ids = lax.broadcasted_iota(jnp.int32, (32, 512), 1)
    driven = rhs_t[...] + jnp.where(ids + row_index * 512 == column, 1.0, 0.0)
    first = jnp.concatenate(
        [jnp.concatenate([top_rhs[2 * i], top_rhs[2 * i + 1]], axis=1) for i in range(4)], axis=0
    )
    first = first + jnp.where(ids[:, :256] == column, 1.0, 0.0)
    solve = dot3(halves(first), (inv_hi[...], inv_lo[...]), NT)
    rest = driven - dot3(halves(solve), (factor_hi[...], factor_lo[...]), NT)
    rhs_out[...] = rest

    @pl.when(row_index == 0)
    def _():
        rhs_out[:, pl.ds(0, 256)] = solve

    for copy in copies:
        copy.wait()


def update(parts, matrix, rhs_t, sources):
    vmem = pl.BlockSpec(memory_space=pltpu.VMEM)
    return pl.pallas_call(
        update_kernel,
        out_shape=(
            jax.ShapeDtypeStruct((512, 1024), jnp.float32),
            jax.ShapeDtypeStruct((32, 512), jnp.float32),
        ),
        in_specs=[vmem] * 11,
        out_specs=(pl.BlockSpec(memory_space=pl.ANY), vmem),
        scratch_shapes=[pltpu.VMEM((512, 1024), jnp.float32), pltpu.SemaphoreType.DMA((NX,))],
        compiler_params=pltpu.CompilerParams(vmem_limit_bytes=24 << 20),
        name="update_trailing",
    )(*parts, matrix, rhs_t, sources)


def shards(matrix, lower_inverse, rhs, sources):
    rhs_t = rhs.T
    parts = spread(matrix, rhs_t, lower_inverse)
    updated, rhs_out = update(parts, matrix, rhs_t, sources.reshape(1, -1))
    return updated, rhs_out.T


def solution(mesh):
    placed = (P("row", "col"), P(), P("row", "col"), P("col"))
    return jax.shard_map(
        shards,
        mesh=mesh,
        in_specs=placed,
        out_specs=(P("row", "col"), P("row", "col")),
        check_vma=False,
    )
```

```python
import functools

import jax
import jax.numpy as jnp
from jax import lax
from jax.experimental import pallas as pl
from jax.experimental.pallas import tpu as pltpu
from jax.sharding import PartitionSpec as P

MESH = pl.DeviceIdType.MESH
NY = 8
NX = 4
NL = 4
NT = ((1,), (1,))
NN = ((1,), (0,))


def coords():
    r = lax.axis_index("row")
    q = lax.axis_index("col")
    return r // 16, (r // 2) % NY, r % 2, q // NL, q % NL


def device(h, y, c, x, l):
    return (h * 16 + y * 2 + c, x * NL + l)


def remote(src, dst, send, recv, target):
    return pltpu.make_async_remote_copy(
        src_ref=src,
        dst_ref=dst,
        send_sem=send,
        recv_sem=recv,
        device_id=device(*target),
        device_id_type=MESH,
    )


def halves(value):
    high = value.astype(jnp.bfloat16)
    return high, (value - high.astype(jnp.float32)).astype(jnp.bfloat16)


def dot3(a, b, contract):
    (ah, al), (bh, bl) = a, b

    def one(u, v):
        return lax.dot_general(u, v, (contract, ((), ())), preferred_element_type=jnp.float32)

    return one(ah, bh) + (one(ah, bl) + one(al, bh))


def spread_kernel(
    matrix, rhs_t, inverse,
    factor, factor_hi, factor_lo, wide_hi, wide_lo, inv_hi, inv_lo, top_rhs,
    left, top, inv,
    t1_send, t_send, s_send, p1_send, p_send,
    t_recv, s_recv, p_recv, local_sem, ready, ready_top, ready_left,
):
    h, y, c, x, l = coords()
    s = 1 - 2 * c
    top_root = (h == 0) & (y == 0) & (c == 0)
    left_root = (x == 0) & (l == 0)
    no = jnp.logical_not
    on = pl.when

    def yy(k):
        return lax.rem(y + k + 2 * NY, NY)

    def xx(k):
        return lax.rem(x + k, NX)

    def ll(k):
        return lax.rem(l + k, NL)

    load_inverse = pltpu.make_async_copy(inverse, inv, local_sem.at[0])
    load_left = pltpu.make_async_copy(matrix.at[:, pl.ds(0, 256)], left, local_sem.at[1])

    @on(top_root)
    def _():
        for a in range(NY):
            for b in range(2):
                pltpu.make_async_copy(
                    matrix.at[pl.ds(b * 128, 128), pl.ds(a * 128, 128)],
                    top.at[a, b, pl.ds(0, 128)], local_sem.at[2],
                ).start()
                pltpu.make_async_copy(
                    rhs_t.at[pl.ds((a // 2) * 8, 8), pl.ds((a % 2) * 128, 128)],
                    top.at[a, b, pl.ds(128, 8)], local_sem.at[2],
                ).start()

    @on(left_root)
    def _():
        load_left.start()

    load_inverse.start()

    barrier = pltpu.get_barrier_semaphore()

    def signal(semaphore, target):
        pl.semaphore_signal(semaphore, inc=1, device_id=device(*target), device_id_type=MESH)

    def rank(v, n):
        return jnp.minimum(v, n - v) * n + v

    partners = []
    for k, slot, back in ((2, 2, 3), (-2, 3, 2), (1, 0, 1), (-1, 1, 0)):
        partners.append((slot, back, (h, yy(k), c, x, l), rank(y, NY) < rank(yy(k), NY)))
    partners.append((10, 10, (1 - h, y, c, x, l), h == 0))
    for k, slot, back in ((2, 8, 8), (1, 7, 9), (3, 9, 7)):
        partners.append((slot, back, (h, y, c, x, ll(k)), l < ll(k)))
    for k, slot, back in ((2, 5, 5), (1, 4, 6), (3, 6, 4)):
        partners.append((slot, back, (h, y, c, xx(k), l), rank(x, NX) < rank(xx(k), NX)))
    partners.append((11, 11, (h, y, 1 - c, x, l), c == 0))
    def is_last(target):
        return sum(target) == 0

    last = is_last((h, y, c, x, l))
    partners = [
        (slot, back, target, no(last) & (early | is_last(target)) if slot in (0, 1, 2, 3, 11) else early)
        for slot, back, target, early in partners
    ]
    earlier = {slot: early for slot, _, _, early in partners}

    near = jnp.minimum(y, NY - y)
    far_top = (h == 0) & (((c == 1) & (y > 0)) | ((c == 0) & (near > 2)))
    far_left = (x > 0) & (l > 0)

    top_last = is_last((0, 0, 0, x, l))

    @on(far_top & top_last)
    def _():
        signal(barrier, (0, 0, 0, x, l))

    @on(top_root & no(last))
    def _():
        for a in (1, 7, 2, 6, 3, 5, 4):
            signal(barrier, (0, a, 1, x, l))
        for a in (3, 5, 4):
            signal(barrier, (0, a, 0, x, l))

    @on(left_root)
    def _():
        for a in range(1, NX):
            for b in range(1, NL):
                signal(barrier, (h, y, c, a, b))

    expected = (
        jnp.where(far_top & no(top_last), 1, 0)
        + jnp.where(far_left, 1, 0)
        + jnp.where(last, 10, 0)
    )
    for slot, back, target, early in partners:
        expected = expected + jnp.where(early, 0, 1)

        @on(early)
        def _():
            signal(barrier, target)

    def settle(who):
        @on(who & (expected > 0))
        def _():
            pl.semaphore_wait(barrier, expected)

        @on(who & far_top & no(top_last))
        def _():
            signal(ready_top.at[y], (0, 0, 0, x, l))

        @on(who & far_left)
        def _():
            signal(ready_left.at[x * NL + l], (h, y, c, 0, 0))

        for slot, back, target, early in partners:
            @on(who & no(early))
            def _():
                signal(ready.at[back], target)

    first_root = top_root & no(last)
    settle(no(first_root))

    def need(slot):
        @on(earlier[slot])
        def _():
            pl.semaphore_wait(ready.at[slot], 1)

    def piece(a, b):
        return left.at[pl.ds(pl.multiple_of(a * 128 + b * 32, 32), 32)]

    def left_scatter(a, b):
        return remote(
            piece(a, b), piece(a, b), p1_send.at[a * NL + b], p_recv.at[a * NL + b], (h, y, c, a, b)
        )

    def left_copy(a, b, j, target):
        return remote(piece(a, b), piece(a, b), p_send.at[j], p_recv.at[a * NL + b], target)

    def left_wait(a, b):
        @on(no(left_root))
        def _():
            left_copy(a, b, 0, (h, y, c, x, l)).wait_recv()

    def top_scatter(a, b):
        return remote(
            top.at[a, b], top.at[a, b], t1_send.at[a * 2 + b], t_recv.at[a], (0, a, b, x, l)
        )

    def top_beside(a):
        return remote(
            top.at[a, 1], top.at[a, 1], t1_send.at[16 + a], t_recv.at[a], (0, 0, 1, x, l)
        )

    def top_copy(a, j, target):
        return remote(top.at[a, c], top.at[a, c], t_send.at[j], t_recv.at[a], target)

    def top_wait(a):
        @on(no(top_root))
        def _():
            top_copy(a, 0, (h, y, c, x, l)).wait_recv()

    def has_all(k):
        return (h == 0) & (yy(k) == 0)

    def top_send(a, j, k):
        @on(no(has_all(k)))
        def _():
            top_copy(a, j, (h, yy(k), c, x, l)).start()

    def sibling(a, half):
        return remote(
            top.at[a, half], top.at[a, half], s_send.at[a], s_recv.at[a], (h, y, 1 - c, x, l)
        )

    beside_root = (h == 0) & (y == 0) & (c == 1)

    def sibling_send(a):
        @on(no(beside_root))
        def _():
            sibling(a, c).start()

    def top_pair(a, slot):
        if slot is not None:
            need(slot)

        @on(no(last))
        def _():
            pl.semaphore_wait(ready_top.at[a], 2 if slot is None else 1)

        for b in range(2):
            top_scatter(a, b).start()

    left_order = [
        (1, 0), (3, 0), (0, 1), (2, 0), (1, 1), (3, 1), (0, 2), (2, 1),
        (1, 2), (3, 2), (0, 3), (2, 2), (1, 3), (3, 3), (2, 3),
    ]

    @on(top_root)
    def _():
        pltpu.make_async_copy(top, top, local_sem.at[2]).wait()
        top_pair(1, 0)
        top_pair(7, 1)
        top_pair(2, 2)
        top_pair(6, 3)
        top_pair(3, None)
        top_pair(5, None)
        top_pair(4, None)
        need(11)
        top_scatter(0, 1).start()
        for a in (6, 2, 1, 7, 3, 5, 4):
            top_beside(a).start()

    settle(first_root)

    @on(left_root)
    def _():
        load_left.wait()
        for a, b in left_order:
            if b == 0:
                need({1: 4, 2: 5, 3: 6}[a])
            elif a == 0:
                need({1: 7, 2: 8, 3: 9}[b])
            else:
                pl.semaphore_wait(ready_left.at[a * NL + b], 1)
            left_scatter(a, b).start()

    load_inverse.wait()
    high, low = halves(inv[...])
    inv_hi[...] = high
    inv_lo[...] = low

    def own_left():
        left_wait(x, l)

        @on(no(left_root))
        def _():
            for slot in (8, 7, 9, 5, 4, 6):
                need(slot)

        for k in (2, 1, 3):
            @on(no((x == 0) & (ll(k) == 0)))
            def _():
                left_copy(x, l, k - 1, (h, y, c, x, ll(k))).start()
        for k in (2, 1, 3):
            @on(no((l == 0) & (xx(k) == 0)))
            def _():
                left_copy(x, l, 2 + k, (h, y, c, xx(k), l)).start()

    def own_top():
        top_wait(y)

        @on(no(top_root))
        def _():
            for slot in (2, 3, 0, 1, 11):
                need(slot)

        for k in (2, -2, 1, -1):
            top_send(y, 3 + k, k)

        @on(h == 0)
        def _():
            need(10)
            top_copy(y, 10, (1, y, c, x, l)).start()

        sibling_send(y)

    def left_relay(m):
        left_wait(x, ll(m))
        for k in (2, 1, 3):
            @on(no((l == 0) & (xx(k) == 0)))
            def _():
                left_copy(x, ll(m), 3 * m + 2 + k, (h, y, c, xx(k), l)).start()

    ahead = yy(-2 * s)
    behind = yy(2 * s)

    def relay_ahead():
        top_wait(ahead)
        top_send(ahead, 3, 2 * s)
        top_send(ahead, 8, s)
        sibling_send(ahead)

    def relay_behind():
        top_wait(behind)
        top_send(behind, 9, -s)
        sibling_send(behind)

    def top_tail(k):
        top_wait(yy(k))
        sibling_send(yy(k))

    inv_halves = (inv_hi[...], inv_lo[...])

    def block(i):
        rows = pl.ds(pl.multiple_of(i * 128, 128), 128)
        part = dot3(halves(left[rows, :]), inv_halves, NT)
        factor[rows, :] = part
        high, low = halves(part)
        factor_hi[rows, :] = high
        factor_lo[rows, :] = low

    def others(k):
        for b in range(NL):
            left_wait(xx(k), b)
        block(xx(k))

    def broad(k):
        a = yy(k)

        @on(no(top_root))
        def _():
            sibling(a, 1 - c).wait_recv()

        chunk = jnp.concatenate([top[a, b, pl.ds(0, 128), :] for b in range(2)], axis=0)
        high, low = halves(dot3(inv_halves, halves(chunk), NN))
        wide_hi[a] = high
        wide_lo[a] = low
        top_rhs[a] = top[a, 0, pl.ds(128, 8), :]

    own_left()
    own_top()
    for m in (1, 3, 2):
        left_relay(m)
    relay_ahead()
    relay_behind()
    block(x)
    top_tail(1)
    top_tail(-1)
    others(1)
    top_tail(3)
    others(3)
    top_tail(-3)
    others(2)
    broad(0)
    top_tail(4)
    for k in (2, -2, 1, -1, 3, -3, 4):
        broad(k)

    for k in (1, 2, 3):
        @on(no((x == 0) & (ll(k) == 0)))
        def _():
            left_copy(x, l, k - 1, (h, y, c, x, l)).wait_send()

        @on(no((l == 0) & (xx(k) == 0)))
        def _():
            for m in range(NL):
                left_copy(x, l, 3 * m + 2 + k, (h, y, c, x, l)).wait_send()

    for j, k in ((1, -2), (2, -1), (4, 1), (5, 2), (3, 2 * s), (8, s), (9, -s)):
        @on(no(has_all(k)))
        def _():
            top_copy(y, j, (h, y, c, x, l)).wait_send()

    @on(no(beside_root))
    def _():
        for a in range(NY):
            sibling(a, c).wait_send()

    @on(h == 0)
    def _():
        top_copy(y, 10, (h, y, c, x, l)).wait_send()

    @on(left_root)
    def _():
        for a, b in left_order:
            left_scatter(a, b).wait_send()

    @on(top_root)
    def _():
        top_scatter(0, 1).wait_send()
        for a in range(1, NY):
            top_beside(a).wait_send()
            for b in range(2):
                top_scatter(a, b).wait_send()


def spread(matrix, rhs_t, inverse, sources=None):
    hbm = lambda value: pltpu.with_memory_space_constraint(value, pltpu.HBM)
    dma = pltpu.SemaphoreType.DMA
    regular = pltpu.SemaphoreType.REGULAR
    f32 = jnp.float32
    b16 = jnp.bfloat16
    return pl.pallas_call(
        spread_kernel,
        out_shape=(
            jax.ShapeDtypeStruct((512, 256), f32),
            jax.ShapeDtypeStruct((512, 256), b16),
            jax.ShapeDtypeStruct((512, 256), b16),
            jax.ShapeDtypeStruct((NY, 256, 128), b16),
            jax.ShapeDtypeStruct((NY, 256, 128), b16),
            jax.ShapeDtypeStruct((256, 256), b16),
            jax.ShapeDtypeStruct((256, 256), b16),
            jax.ShapeDtypeStruct((NY, 8, 128), f32),
        ),
        in_specs=[pl.BlockSpec(memory_space=pltpu.HBM)] * 3,
        out_specs=(pl.BlockSpec(memory_space=pltpu.VMEM),) * 8,
        scratch_shapes=[
            pltpu.VMEM((512, 256), f32),
            pltpu.VMEM((NY, 2, 136, 128), f32),
            pltpu.VMEM((256, 256), f32),
            dma((24,)), dma((11,)), dma((8,)), dma((16,)), dma((15,)),
            dma((8,)), dma((8,)), dma((16,)), dma((3,)),
            regular((12,)), regular((8,)), regular((16,)),
        ],
        compiler_params=pltpu.CompilerParams(
            collective_id=0, has_side_effects=True, vmem_limit_bytes=24 << 20
        ),
        name="spread_panel",
    )(hbm(matrix), hbm(rhs_t), hbm(inverse))


def update_kernel(
    factor, factor_hi, factor_lo, wide_hi, wide_lo, inv_hi, inv_lo, top_rhs,
    matrix, rhs_t, sources, updated, rhs_out, result, out_sem,
):
    row_index = lax.axis_index("row")
    col_index = lax.axis_index("col")
    wide = tuple(
        jnp.concatenate([ref[i] for i in range(NY)], axis=1) for ref in (wide_hi, wide_lo)
    )
    copies = []
    for i in range(NX):
        rows = pl.ds(i * 128, 128)
        product = dot3((factor_hi[rows, :], factor_lo[rows, :]), wide, NN)
        held = matrix[rows, :]
        result[rows, :] = held - product

        @pl.when(col_index == 0)
        def _():
            result[rows, pl.ds(0, 256)] = factor[rows, :]

        if i < 2:
            @pl.when(row_index == 0)
            def _():
                result[rows, :] = held

        copy = pltpu.make_async_copy(result.at[rows], updated.at[rows], out_sem.at[i])
        copy.start()
        copies.append(copy)

    spare = jnp.broadcast_to(sources[...].astype(jnp.float32), (32, 32))
    eye = lax.broadcasted_iota(jnp.int32, (32, 32), 0) == lax.broadcasted_iota(jnp.int32, (32, 32), 1)
    column = jnp.sum(jnp.where(eye, spare, 0.0), axis=1, keepdims=True).astype(jnp.int32)
    ids = lax.broadcasted_iota(jnp.int32, (32, 512), 1)
    driven = rhs_t[...] + jnp.where(ids + row_index * 512 == column, 1.0, 0.0)
    first = jnp.concatenate(
        [jnp.concatenate([top_rhs[2 * i], top_rhs[2 * i + 1]], axis=1) for i in range(4)], axis=0
    )
    first = first + jnp.where(ids[:, :256] == column, 1.0, 0.0)
    solve = dot3(halves(first), (inv_hi[...], inv_lo[...]), NT)
    rest = driven - dot3(halves(solve), (factor_hi[...], factor_lo[...]), NT)
    rhs_out[...] = rest

    @pl.when(row_index == 0)
    def _():
        rhs_out[:, pl.ds(0, 256)] = solve

    for copy in copies:
        copy.wait()


def update(parts, matrix, rhs_t, sources):
    vmem = pl.BlockSpec(memory_space=pltpu.VMEM)
    return pl.pallas_call(
        update_kernel,
        out_shape=(
            jax.ShapeDtypeStruct((512, 1024), jnp.float32),
            jax.ShapeDtypeStruct((32, 512), jnp.float32),
        ),
        in_specs=[vmem] * 11,
        out_specs=(pl.BlockSpec(memory_space=pl.ANY), vmem),
        scratch_shapes=[pltpu.VMEM((512, 1024), jnp.float32), pltpu.SemaphoreType.DMA((NX,))],
        compiler_params=pltpu.CompilerParams(vmem_limit_bytes=24 << 20),
        name="update_trailing",
    )(*parts, matrix, rhs_t, sources)


def shards(matrix, lower_inverse, rhs, sources):
    rhs_t = rhs.T
    parts = spread(matrix, rhs_t, lower_inverse)
    updated, rhs_out = update(parts, matrix, rhs_t, sources.reshape(1, -1))
    return updated, rhs_out.T


def solution(mesh):
    placed = (P("row", "col"), P(), P("row", "col"), P("col"))
    return jax.shard_map(
        shards,
        mesh=mesh,
        in_specs=placed,
        out_specs=(P("row", "col"), P("row", "col")),
        check_vma=False,
    )
```

```python
import functools

import jax
import jax.numpy as jnp
from jax import lax
from jax.experimental import pallas as pl
from jax.experimental.pallas import tpu as pltpu
from jax.sharding import PartitionSpec as P

MESH = pl.DeviceIdType.MESH
NY = 8
NX = 4
NL = 4
NT = ((1,), (1,))
NN = ((1,), (0,))


def coords():
    r = lax.axis_index("row")
    q = lax.axis_index("col")
    return r // 16, (r // 2) % NY, r % 2, q // NL, q % NL


def device(h, y, c, x, l):
    return (h * 16 + y * 2 + c, x * NL + l)


def remote(src, dst, send, recv, target):
    return pltpu.make_async_remote_copy(
        src_ref=src,
        dst_ref=dst,
        send_sem=send,
        recv_sem=recv,
        device_id=device(*target),
        device_id_type=MESH,
    )


def halves(value):
    high = value.astype(jnp.bfloat16)
    return high, (value - high.astype(jnp.float32)).astype(jnp.bfloat16)


def dot3(a, b, contract):
    (ah, al), (bh, bl) = a, b

    def one(u, v):
        return lax.dot_general(u, v, (contract, ((), ())), preferred_element_type=jnp.float32)

    return one(ah, bh) + (one(ah, bl) + one(al, bh))


def spread_kernel(
    matrix, rhs_t, inverse,
    factor, factor_hi, factor_lo, wide_hi, wide_lo, inv_hi, inv_lo, top_rhs,
    left, top, inv,
    t1_send, t_send, s_send, p1_send, p_send,
    t_recv, s_recv, p_recv, local_sem, ready, ready_top, ready_left,
):
    h, y, c, x, l = coords()
    s = 1 - 2 * c
    top_root = (h == 0) & (y == 0) & (c == 0)
    left_root = (x == 0) & (l == 0)
    no = jnp.logical_not
    on = pl.when

    def yy(k):
        return lax.rem(y + k + 2 * NY, NY)

    def xx(k):
        return lax.rem(x + k, NX)

    def ll(k):
        return lax.rem(l + k, NL)

    load_inverse = pltpu.make_async_copy(inverse, inv, local_sem.at[0])
    load_left = pltpu.make_async_copy(matrix.at[:, pl.ds(0, 256)], left, local_sem.at[1])

    @on(top_root)
    def _():
        for a in range(NY):
            for b in range(2):
                pltpu.make_async_copy(
                    matrix.at[pl.ds(b * 128, 128), pl.ds(a * 128, 128)],
                    top.at[a, b, pl.ds(0, 128)], local_sem.at[2],
                ).start()
                pltpu.make_async_copy(
                    rhs_t.at[pl.ds((a // 2) * 8, 8), pl.ds((a % 2) * 128, 128)],
                    top.at[a, b, pl.ds(128, 8)], local_sem.at[2],
                ).start()

    @on(left_root)
    def _():
        load_left.start()

    load_inverse.start()

    barrier = pltpu.get_barrier_semaphore()

    def signal(semaphore, target):
        pl.semaphore_signal(semaphore, inc=1, device_id=device(*target), device_id_type=MESH)

    def rank(v, n):
        return jnp.minimum(v, n - v) * n + v

    partners = []
    for k, slot, back in ((2, 2, 3), (-2, 3, 2), (1, 0, 1), (-1, 1, 0)):
        partners.append((slot, back, (h, yy(k), c, x, l), rank(y, NY) < rank(yy(k), NY)))
    partners.append((10, 10, (1 - h, y, c, x, l), h == 0))
    for k, slot, back in ((2, 8, 8), (1, 7, 9), (3, 9, 7)):
        partners.append((slot, back, (h, y, c, x, ll(k)), l < ll(k)))
    for k, slot, back in ((2, 5, 5), (1, 4, 6), (3, 6, 4)):
        partners.append((slot, back, (h, y, c, xx(k), l), rank(x, NX) < rank(xx(k), NX)))
    partners.append((11, 11, (h, y, 1 - c, x, l), c == 0))
    def is_last(target):
        return sum(target) == 0

    last = is_last((h, y, c, x, l))
    partners = [
        (slot, back, target, no(last) & (early | is_last(target)) if slot in (0, 1, 2, 3, 11) else early)
        for slot, back, target, early in partners
    ]
    earlier = {slot: early for slot, _, _, early in partners}

    near = jnp.minimum(y, NY - y)
    far_top = (h == 0) & (((c == 1) & (y > 0)) | ((c == 0) & (near > 2)))
    far_left = (x > 0) & (l > 0)

    top_last = is_last((0, 0, 0, x, l))

    @on(far_top & top_last)
    def _():
        signal(barrier, (0, 0, 0, x, l))

    @on(top_root & no(last))
    def _():
        for a in (1, 7, 2, 6, 3, 5, 4):
            signal(barrier, (0, a, 1, x, l))
        for a in (3, 5, 4):
            signal(barrier, (0, a, 0, x, l))

    @on(left_root)
    def _():
        for a in range(1, NX):
            for b in range(1, NL):
                signal(barrier, (h, y, c, a, b))

    expected = (
        jnp.where(far_top & no(top_last), 1, 0)
        + jnp.where(far_left, 1, 0)
        + jnp.where(last, 10, 0)
    )
    for slot, back, target, early in partners:
        expected = expected + jnp.where(early, 0, 1)

        @on(early)
        def _():
            signal(barrier, target)

    def settle(who):
        @on(who & (expected > 0))
        def _():
            pl.semaphore_wait(barrier, expected)

        @on(who & far_top & no(top_last))
        def _():
            signal(ready_top.at[y], (0, 0, 0, x, l))

        @on(who & far_left)
        def _():
            signal(ready_left.at[x * NL + l], (h, y, c, 0, 0))

        for slot, back, target, early in partners:
            @on(who & no(early))
            def _():
                signal(ready.at[back], target)

    first_root = top_root & no(last)
    settle(no(first_root))

    def need(slot):
        @on(earlier[slot])
        def _():
            pl.semaphore_wait(ready.at[slot], 1)

    def piece(a, b):
        return left.at[pl.ds(pl.multiple_of(a * 128 + b * 32, 32), 32)]

    def left_scatter(a, b):
        return remote(
            piece(a, b), piece(a, b), p1_send.at[a * NL + b], p_recv.at[a * NL + b], (h, y, c, a, b)
        )

    def left_copy(a, b, j, target):
        return remote(piece(a, b), piece(a, b), p_send.at[j], p_recv.at[a * NL + b], target)

    def left_wait(a, b):
        @on(no(left_root))
        def _():
            left_copy(a, b, 0, (h, y, c, x, l)).wait_recv()

    def top_scatter(a, b):
        return remote(
            top.at[a, b], top.at[a, b], t1_send.at[a * 2 + b], t_recv.at[a], (0, a, b, x, l)
        )

    def top_beside(a):
        return remote(
            top.at[a, 1], top.at[a, 1], t1_send.at[16 + a], t_recv.at[a], (0, 0, 1, x, l)
        )

    def top_copy(a, j, target):
        return remote(top.at[a, c], top.at[a, c], t_send.at[j], t_recv.at[a], target)

    def top_wait(a):
        @on(no(top_root))
        def _():
            top_copy(a, 0, (h, y, c, x, l)).wait_recv()

    def has_all(k):
        return (h == 0) & (yy(k) == 0)

    def top_send(a, j, k):
        @on(no(has_all(k)))
        def _():
            top_copy(a, j, (h, yy(k), c, x, l)).start()

    def sibling(a, half):
        return remote(
            top.at[a, half], top.at[a, half], s_send.at[a], s_recv.at[a], (h, y, 1 - c, x, l)
        )

    root_chip = (h == 0) & (y == 0)
    beside_root = (h == 0) & (y == 0) & (c == 1)

    def sibling_send(a):
        @on(no(beside_root))
        def _():
            sibling(a, c).start()

    def top_pair(a, slot):
        if slot is not None:
            need(slot)

        @on(no(last))
        def _():
            pl.semaphore_wait(ready_top.at[a], 2 if slot is None else 1)

        for b in range(2):
            top_scatter(a, b).start()

    left_order = [
        (1, 0), (3, 0), (0, 1), (2, 0), (1, 1), (3, 1), (0, 2), (2, 1),
        (1, 2), (3, 2), (0, 3), (2, 2), (1, 3), (3, 3), (2, 3),
    ]

    @on(top_root)
    def _():
        pltpu.make_async_copy(top, top, local_sem.at[2]).wait()
        top_pair(1, 0)
        top_pair(7, 1)
        top_pair(2, 2)
        top_pair(6, 3)
        top_pair(3, None)
        top_pair(5, None)
        top_pair(4, None)
        need(11)
        top_scatter(0, 1).start()
        for a in (6, 2, 1, 7, 3, 5, 4):
            top_beside(a).start()

    settle(first_root)

    @on(left_root)
    def _():
        load_left.wait()
        for a, b in left_order:
            if b == 0:
                need({1: 4, 2: 5, 3: 6}[a])
            elif a == 0:
                need({1: 7, 2: 8, 3: 9}[b])
            else:
                pl.semaphore_wait(ready_left.at[a * NL + b], 1)
            left_scatter(a, b).start()

    load_inverse.wait()
    high, low = halves(inv[...])
    inv_hi[...] = high
    inv_lo[...] = low

    def own_left():
        left_wait(x, l)

        @on(no(left_root))
        def _():
            for slot in (8, 7, 9, 5, 4, 6):
                need(slot)

        for k in (2, 1, 3):
            @on(no((x == 0) & (ll(k) == 0)))
            def _():
                left_copy(x, l, k - 1, (h, y, c, x, ll(k))).start()
        for k in (2, 1, 3):
            @on(no((l == 0) & (xx(k) == 0)))
            def _():
                left_copy(x, l, 2 + k, (h, y, c, xx(k), l)).start()

    def own_top():
        top_wait(y)

        @on(no(top_root))
        def _():
            for slot in (2, 3, 0, 1, 11):
                need(slot)

        @on((h == 0) & no(root_chip))
        def _():
            need(10)
            top_copy(y, 10, (1, y, c, x, l)).start()

        for k in (2, -2, 1, -1):
            top_send(y, 3 + k, k)

        @on(root_chip)
        def _():
            need(10)
            top_copy(y, 10, (1, y, c, x, l)).start()

        sibling_send(y)

    def left_relay(m):
        left_wait(x, ll(m))
        for k in (2, 1, 3):
            @on(no((l == 0) & (xx(k) == 0)))
            def _():
                left_copy(x, ll(m), 3 * m + 2 + k, (h, y, c, xx(k), l)).start()

    ahead = yy(-2 * s)
    behind = yy(2 * s)

    def relay_ahead():
        top_wait(ahead)
        top_send(ahead, 3, 2 * s)
        top_send(ahead, 8, s)
        sibling_send(ahead)

    def relay_behind():
        top_wait(behind)
        top_send(behind, 9, -s)
        sibling_send(behind)

    def top_tail(k):
        top_wait(yy(k))
        sibling_send(yy(k))

    inv_halves = (inv_hi[...], inv_lo[...])

    def block(i):
        rows = pl.ds(pl.multiple_of(i * 128, 128), 128)
        part = dot3(halves(left[rows, :]), inv_halves, NT)
        factor[rows, :] = part
        high, low = halves(part)
        factor_hi[rows, :] = high
        factor_lo[rows, :] = low

    def others(k):
        for b in range(NL):
            left_wait(xx(k), b)
        block(xx(k))

    def broad(k):
        a = yy(k)

        @on(no(top_root))
        def _():
            sibling(a, 1 - c).wait_recv()

        chunk = jnp.concatenate([top[a, b, pl.ds(0, 128), :] for b in range(2)], axis=0)
        high, low = halves(dot3(inv_halves, halves(chunk), NN))
        wide_hi[a] = high
        wide_lo[a] = low
        top_rhs[a] = top[a, 0, pl.ds(128, 8), :]

    own_left()
    own_top()
    for m in (1, 3, 2):
        left_relay(m)
    relay_ahead()
    relay_behind()
    block(x)
    top_tail(1)
    top_tail(-1)
    others(1)
    top_tail(3)
    others(3)
    top_tail(-3)
    others(2)
    broad(0)
    top_tail(4)
    for k in (2, -2, 1, -1, 3, -3, 4):
        broad(k)

    for k in (1, 2, 3):
        @on(no((x == 0) & (ll(k) == 0)))
        def _():
            left_copy(x, l, k - 1, (h, y, c, x, l)).wait_send()

        @on(no((l == 0) & (xx(k) == 0)))
        def _():
            for m in range(NL):
                left_copy(x, l, 3 * m + 2 + k, (h, y, c, x, l)).wait_send()

    for j, k in ((1, -2), (2, -1), (4, 1), (5, 2), (3, 2 * s), (8, s), (9, -s)):
        @on(no(has_all(k)))
        def _():
            top_copy(y, j, (h, y, c, x, l)).wait_send()

    @on(no(beside_root))
    def _():
        for a in range(NY):
            sibling(a, c).wait_send()

    @on(h == 0)
    def _():
        top_copy(y, 10, (h, y, c, x, l)).wait_send()

    @on(left_root)
    def _():
        for a, b in left_order:
            left_scatter(a, b).wait_send()

    @on(top_root)
    def _():
        top_scatter(0, 1).wait_send()
        for a in range(1, NY):
            top_beside(a).wait_send()
            for b in range(2):
                top_scatter(a, b).wait_send()


def spread(matrix, rhs_t, inverse, sources=None):
    hbm = lambda value: pltpu.with_memory_space_constraint(value, pltpu.HBM)
    dma = pltpu.SemaphoreType.DMA
    regular = pltpu.SemaphoreType.REGULAR
    f32 = jnp.float32
    b16 = jnp.bfloat16
    return pl.pallas_call(
        spread_kernel,
        out_shape=(
            jax.ShapeDtypeStruct((512, 256), f32),
            jax.ShapeDtypeStruct((512, 256), b16),
            jax.ShapeDtypeStruct((512, 256), b16),
            jax.ShapeDtypeStruct((NY, 256, 128), b16),
            jax.ShapeDtypeStruct((NY, 256, 128), b16),
            jax.ShapeDtypeStruct((256, 256), b16),
            jax.ShapeDtypeStruct((256, 256), b16),
            jax.ShapeDtypeStruct((NY, 8, 128), f32),
        ),
        in_specs=[pl.BlockSpec(memory_space=pltpu.HBM)] * 3,
        out_specs=(pl.BlockSpec(memory_space=pltpu.VMEM),) * 8,
        scratch_shapes=[
            pltpu.VMEM((512, 256), f32),
            pltpu.VMEM((NY, 2, 136, 128), f32),
            pltpu.VMEM((256, 256), f32),
            dma((24,)), dma((11,)), dma((8,)), dma((16,)), dma((15,)),
            dma((8,)), dma((8,)), dma((16,)), dma((3,)),
            regular((12,)), regular((8,)), regular((16,)),
        ],
        compiler_params=pltpu.CompilerParams(
            collective_id=0, has_side_effects=True, vmem_limit_bytes=24 << 20
        ),
        name="spread_panel",
    )(hbm(matrix), hbm(rhs_t), hbm(inverse))


def update_kernel(
    factor, factor_hi, factor_lo, wide_hi, wide_lo, inv_hi, inv_lo, top_rhs,
    matrix, rhs_t, sources, updated, rhs_out, result, out_sem,
):
    row_index = lax.axis_index("row")
    col_index = lax.axis_index("col")
    wide = tuple(
        jnp.concatenate([ref[i] for i in range(NY)], axis=1) for ref in (wide_hi, wide_lo)
    )
    copies = []
    for i in range(NX):
        rows = pl.ds(i * 128, 128)
        product = dot3((factor_hi[rows, :], factor_lo[rows, :]), wide, NN)
        held = matrix[rows, :]
        result[rows, :] = held - product

        @pl.when(col_index == 0)
        def _():
            result[rows, pl.ds(0, 256)] = factor[rows, :]

        if i < 2:
            @pl.when(row_index == 0)
            def _():
                result[rows, :] = held

        copy = pltpu.make_async_copy(result.at[rows], updated.at[rows], out_sem.at[i])
        copy.start()
        copies.append(copy)

    spare = jnp.broadcast_to(sources[...].astype(jnp.float32), (32, 32))
    eye = lax.broadcasted_iota(jnp.int32, (32, 32), 0) == lax.broadcasted_iota(jnp.int32, (32, 32), 1)
    column = jnp.sum(jnp.where(eye, spare, 0.0), axis=1, keepdims=True).astype(jnp.int32)
    ids = lax.broadcasted_iota(jnp.int32, (32, 512), 1)
    driven = rhs_t[...] + jnp.where(ids + row_index * 512 == column, 1.0, 0.0)
    first = jnp.concatenate(
        [jnp.concatenate([top_rhs[2 * i], top_rhs[2 * i + 1]], axis=1) for i in range(4)], axis=0
    )
    first = first + jnp.where(ids[:, :256] == column, 1.0, 0.0)
    solve = dot3(halves(first), (inv_hi[...], inv_lo[...]), NT)
    rest = driven - dot3(halves(solve), (factor_hi[...], factor_lo[...]), NT)
    rhs_out[...] = rest

    @pl.when(row_index == 0)
    def _():
        rhs_out[:, pl.ds(0, 256)] = solve

    for copy in copies:
        copy.wait()


def update(parts, matrix, rhs_t, sources):
    vmem = pl.BlockSpec(memory_space=pltpu.VMEM)
    return pl.pallas_call(
        update_kernel,
        out_shape=(
            jax.ShapeDtypeStruct((512, 1024), jnp.float32),
            jax.ShapeDtypeStruct((32, 512), jnp.float32),
        ),
        in_specs=[vmem] * 11,
        out_specs=(pl.BlockSpec(memory_space=pl.ANY), vmem),
        scratch_shapes=[pltpu.VMEM((512, 1024), jnp.float32), pltpu.SemaphoreType.DMA((NX,))],
        compiler_params=pltpu.CompilerParams(vmem_limit_bytes=24 << 20),
        name="update_trailing",
    )(*parts, matrix, rhs_t, sources)


def shards(matrix, lower_inverse, rhs, sources):
    rhs_t = rhs.T
    parts = spread(matrix, rhs_t, lower_inverse)
    updated, rhs_out = update(parts, matrix, rhs_t, sources.reshape(1, -1))
    return updated, rhs_out.T


def solution(mesh):
    placed = (P("row", "col"), P(), P("row", "col"), P("col"))
    return jax.shard_map(
        shards,
        mesh=mesh,
        in_specs=placed,
        out_specs=(P("row", "col"), P("row", "col")),
        check_vma=False,
    )
```
